32 devices in a mesh: band: 8 (over z, y), grid: 4 (over x, core).
Axes of the slice: x: 2, y: 2, z: 4, core: 2. Of those that a mesh axis runs over, the one named last changes fastest.
Arguments:
- orbitals: bfloat16 [512, 64, 4096], P('band', 'grid'), may hold values from -6 to 6
- picks: int32 [1], replicated, may hold values from 0 to 511
Outputs:
- exchange_vectors: bfloat16 [512, 64, 4096], P('band', 'grid')
- gram: float32 [512, 512], P('band')
The draws below stay inside these ranges and needn't reach their ends.
All inputs are finite; a program needn't handle non-finite values.
Results may differ from the reference program's by a relative error of at most 0.00085.
Values may be sent and summed in bfloat16 or wider, within the bound.
A program may use at most 192 MiB of HBM per device.

```python
import jax
import jax.numpy as jnp
from jax import lax

NB = 512
NG = 64
NPICK = 1
NPTS = 262144


def levels(rng, extent, split, low, top_value):
    def one(axis_at, parts):
        draws = jax.random.uniform(jax.random.fold_in(jax.random.fold_in(rng, 6), axis_at), (parts,), jnp.float32, low / len(split), top_value / len(split))
        return jnp.repeat(jnp.exp(draws), extent[axis_at] // parts).reshape((-1,) + (1,) * (len(extent) - axis_at - 1))

    factor_of = one(*split[0])
    for cut in split[1:]:
        factor_of = factor_of * one(*cut)
    return factor_of


def centred(own_key, shape, deviation, bound, cuts=(), kind=jnp.bfloat16):
    array = jax.random.normal(own_key, shape, jnp.float32) * deviation
    if len(cuts) > 0:
        array = levels(own_key, shape, cuts, -0.22, 0.18) * array
    return jnp.clip(array, min=-bound, max=bound).astype(kind)


def setup_inputs(seed: int = 0) -> dict:
    key_of = jax.random.split(jax.random.key(seed), 3)
    return {
        "orbitals": centred(key_of[0], (NB, NG, NG * NG), 1.0, 6.0, ((0, 8), (1, 4))),
        "picks": jax.random.randint(key_of[1], (NPICK,), 0, NB).astype(jnp.int32),
    }


KERNEL_SCALE = 128.0


def kernel_table():
    frequency = jnp.arange(NG, dtype=jnp.int32)
    folded = jnp.minimum(frequency, NG - frequency).astype(jnp.float32)
    square = folded * folded
    summed = square[:, None, None] + square[None, :, None] + square[None, None, :]
    return jnp.where(summed > 0, KERNEL_SCALE / jnp.maximum(summed, 1.0), 0.0)


def reference(orbitals, picks):
    cubes = orbitals.reshape(NB, NG, NG, NG)
    chosen = jnp.take(cubes, picks, axis=0).astype(jnp.float32)
    table = kernel_table()

    def block_vectors(rows):
        values = rows.astype(jnp.float32)
        accumulated = jnp.zeros(values.shape, jnp.float32)
        for position in range(NPICK):
            partner = chosen[position]
            density = values * partner[None]
            spectrum = jnp.fft.fftn(density, axes=(1, 2, 3))
            potential = jnp.real(jnp.fft.ifftn(spectrum * table[None], axes=(1, 2, 3)))
            accumulated = accumulated - potential * partner[None]
        return accumulated.astype(jnp.bfloat16)

    block_rows = min(NB, 64)
    vectors = lax.map(block_vectors, cubes.reshape(NB // block_rows, block_rows, NG, NG, NG))
    vectors = vectors.reshape(NB, NG, NG * NG)
    flat_orbitals = orbitals.reshape(NB, NPTS)
    flat_vectors = vectors.reshape(NB, NPTS)
    gram = lax.dot_general(flat_orbitals, flat_vectors, (((1,), (1,)), ((), ())), preferred_element_type=jnp.float32) / NPTS
    return vectors, gram
```

```python
import math

import jax
import jax.numpy as jnp
from jax import lax
from jax.experimental import pallas as pl
from jax.experimental.pallas import tpu as pltpu
from jax.sharding import PartitionSpec as P

NG = 64
NPTS = 262144
KERNEL_SCALE = 128.0
BF = jnp.bfloat16
F32 = jnp.float32


def spread(value, axis, source):
    kept = jnp.where(lax.axis_index(axis) == source, value, 0).astype(value.dtype)
    return lax.psum(kept, axis)


def cas_matrix(length):
    products = (
        jnp.arange(length, dtype=jnp.int32)[:, None]
        * jnp.arange(length, dtype=jnp.int32)[None, :]
        % length
    )
    angles = products.astype(F32) * (2.0 * math.pi / length)
    return jnp.cos(angles) + jnp.sin(angles)


def halves(value):
    high = value.astype(BF)
    return high, (value - high.astype(F32)).astype(BF)


def matrix_halves(value):
    high = lax.reduce_precision(value, 8, 7)
    return high.astype(BF), (value - high).astype(BF)


def kernel_table():
    frequency = jnp.arange(NG, dtype=jnp.int32)
    folded = jnp.minimum(frequency, NG - frequency).astype(F32)
    square = folded * folded
    summed = square[:, None, None] + square[None, :, None] + square[None, None, :]
    table = jnp.where(summed > 0, KERNEL_SCALE / NPTS / jnp.maximum(summed, 1.0), 0.0)
    return jnp.concatenate([table, table], axis=2)


def dot(a, b):
    return jnp.dot(a, b, preferred_element_type=F32)


def solve_body(slabs, rows, orb, partner, table, left_hi, left_lo, right_hi, right_lo, out, work):
    def along_rows(value):
        high, low = halves(value)
        both = dot(left_hi[...], jnp.concatenate([high, low], axis=1))
        return both[:, :128] + both[:, 128:] + dot(left_lo[...], high)

    def along_lanes(value):
        high, low = halves(value)
        return dot(jnp.concatenate([high, low], axis=1), right_hi[...]) + dot(high, right_lo[...])

    for slab in range(slabs):
        @pl.loop(0, rows // 4, unroll=2)
        def _(i):
            at = pl.ds(i * 4, 4)
            x = slab * rows + i * 4
            field = orb[slab, 0, at].astype(F32) * partner[pl.ds(x, 4)].astype(F32)
            field = along_rows(along_lanes(field.reshape(256, 128)))
            work[pl.ds(x, 4)] = field.reshape(4, NG, 128)

    @pl.loop(0, NG // 8)
    def _(i):
        at = pl.ds(pl.multiple_of(i * 8, 8), 8)
        planes = jnp.swapaxes(work[:, at, :], 0, 1)
        done = []
        for part in range(2):
            field = planes[part * 4:part * 4 + 4].reshape(256, 128)
            field = along_rows(field) * table[pl.ds(i * 8 + part * 4, 4)].reshape(256, 128)
            done.append(along_rows(field).reshape(4, NG, 128))
        work[:, at, :] = jnp.swapaxes(jnp.concatenate(done, axis=0), 0, 1)

    for slab in range(slabs):
        @pl.loop(0, rows // 4, unroll=2)
        def _(i):
            x = slab * rows + i * 4
            field = along_lanes(along_rows(work[pl.ds(x, 4)].reshape(256, 128)))
            field = field.reshape(4, NG, 128) * partner[pl.ds(x, 4)].astype(F32)
            out[slab, 0, pl.ds(i * 4, 4)] = (-field).astype(BF)


def solve(pairs, partner):
    slabs, count, rows = pairs.shape[:3]
    matrix = cas_matrix(NG)
    left = matrix_halves(jnp.kron(jnp.eye(4, dtype=F32), matrix))
    right = matrix_halves(jnp.kron(jnp.eye(2, dtype=F32), matrix))
    right_hi = jnp.concatenate([right[0], right[0]], axis=0)
    block = pl.BlockSpec((slabs, 1, rows, NG, 128), lambda i: (0, i, 0, 0, 0))
    whole = lambda array: pl.BlockSpec(array.shape, lambda i: (0,) * array.ndim)
    fixed = (partner, kernel_table(), left[0], left[1], right_hi, right[1])
    return pl.pallas_call(
        lambda *refs: solve_body(slabs, rows, *refs),
        grid=(count,),
        in_specs=[block] + [whole(a) for a in fixed],
        out_specs=block,
        out_shape=jax.ShapeDtypeStruct(pairs.shape, BF),
        scratch_shapes=[pltpu.VMEM((NG, NG, 128), F32)],
        compiler_params=pltpu.CompilerParams(vmem_limit_bytes=48 * 1024 * 1024),
        cost_estimate=pl.CostEstimate(
            flops=count * 60 * NG * NG * 128 * 256, bytes_accessed=4 * pairs.size, transcendentals=0
        ),
    )(pairs, *fixed)


def gram_body(left, right, out):
    @pl.when(pl.program_id(0) == 0)
    def _():
        out[...] = jnp.zeros_like(out)

    size = out.shape[0]
    a = left[:, 0].reshape(size, left.shape[3])
    b = right[:, 0].reshape(size, right.shape[3])
    out[...] += lax.dot_general(a, b, (((1,), (1,)), ((), ())), preferred_element_type=F32)


def gram_product(left, right):
    shares, planes, bands, points = left.shape
    size = shares * bands
    if bands % 16 or points % 128:
        return jnp.einsum("gxbk,hxck->gbhc", left, right, preferred_element_type=F32).reshape(size, size)
    block = pl.BlockSpec((shares, 1, bands, points), lambda i: (0, i, 0, 0))
    return pl.pallas_call(
        gram_body,
        grid=(planes,),
        in_specs=[block, block],
        out_specs=pl.BlockSpec((size, size), lambda i: (0, 0)),
        out_shape=jax.ShapeDtypeStruct((size, size), F32),
        compiler_params=pltpu.CompilerParams(vmem_limit_bytes=32 * 1024 * 1024),
        cost_estimate=pl.CostEstimate(
            flops=2 * size * size * planes * points, bytes_accessed=4 * left.size, transcendentals=0
        ),
    )(left, right)


def to_shares(array):
    shares = lax.axis_size("band")
    bands, planes, square = array.shape
    cut = array.reshape(bands, planes, shares, square // shares).transpose(2, 1, 0, 3)
    return lax.all_to_all(cut, "band", split_axis=0, concat_axis=0)


def per_device(orbitals, picks):
    bands, planes, square = orbitals.shape
    groups = lax.axis_size("grid")
    pairs = bands // groups // 2
    target = picks[0]
    mine = lax.dynamic_index_in_dim(orbitals, target % bands, 0, keepdims=False)
    slab = spread(mine, "band", target // bands).reshape(planes, NG, NG)
    partner = lax.all_gather(jnp.concatenate([slab, slab], axis=2), "grid", axis=0, tiled=True)

    paired = orbitals.reshape(groups, pairs, 2, planes, NG, NG).transpose(0, 1, 3, 4, 2, 5)
    paired = paired.reshape(groups, pairs, planes, NG, 128)
    cubes = lax.all_to_all(paired, "grid", split_axis=0, concat_axis=0)
    spread_orbitals = to_shares(orbitals)
    solved = solve(cubes, partner)
    back = lax.all_to_all(solved, "grid", split_axis=0, concat_axis=0)
    vectors = back.reshape(groups, pairs, planes, NG, 2, NG).transpose(0, 1, 4, 2, 3, 5)
    vectors = vectors.reshape(bands, planes, square)
    spread_vectors = to_shares(vectors)
    product = gram_product(spread_orbitals, spread_vectors)
    partial_rows = lax.psum_scatter(product * (1.0 / NPTS), "band", scatter_dimension=0, tiled=True)
    gram = lax.psum(partial_rows, "grid")
    return (vectors, gram)


def solution(mesh):
    return jax.shard_map(
        per_device,
        mesh=mesh,
        in_specs=(P("band", "grid", None), P()),
        out_specs=(P("band", "grid", None), P("band", None)),
        check_vma=False,
    )
```

```python
import math

import jax
import jax.numpy as jnp
from jax import lax
from jax.experimental import pallas as pl
from jax.experimental.pallas import tpu as pltpu
from jax.sharding import PartitionSpec as P

NG = 64
NPTS = 262144
KERNEL_SCALE = 128.0
BF = jnp.bfloat16
F32 = jnp.float32


def spread(value, axis, source):
    kept = jnp.where(lax.axis_index(axis) == source, value, 0).astype(value.dtype)
    return lax.psum(kept, axis)


def cas_matrix(length):
    products = (
        jnp.arange(length, dtype=jnp.int32)[:, None]
        * jnp.arange(length, dtype=jnp.int32)[None, :]
        % length
    )
    angles = products.astype(F32) * (2.0 * math.pi / length)
    return jnp.cos(angles) + jnp.sin(angles)


def halves(value):
    high = value.astype(BF)
    return high, (value - high.astype(F32)).astype(BF)


def matrix_halves(value):
    high = lax.reduce_precision(value, 8, 7)
    return high.astype(BF), (value - high).astype(BF)


def kernel_table():
    frequency = jnp.arange(NG, dtype=jnp.int32)
    folded = jnp.minimum(frequency, NG - frequency).astype(F32)
    square = folded * folded
    summed = square[:, None, None] + square[None, :, None] + square[None, None, :]
    table = jnp.where(summed > 0, KERNEL_SCALE / NPTS / jnp.maximum(summed, 1.0), 0.0)
    return jnp.concatenate([table, table], axis=2)


def dot(a, b):
    return jnp.dot(a, b, preferred_element_type=F32)


def solve_body(slabs, rows, orb, partner, table, left_hi, left_lo, right_hi, right_lo, out, work):
    def along_rows(value):
        high, low = halves(value)
        both = dot(left_hi[...], jnp.concatenate([high, low], axis=1))
        return both[:, :128] + both[:, 128:] + dot(left_lo[...], high)

    def along_lanes(value):
        high, low = halves(value)
        return dot(jnp.concatenate([high, low], axis=1), right_hi[...]) + dot(high, right_lo[...])

    for slab in range(slabs):
        @pl.loop(0, rows // 4, unroll=2)
        def _(i):
            at = pl.ds(i * 4, 4)
            x = slab * rows + i * 4
            field = orb[slab, 0, at].astype(F32) * partner[pl.ds(x, 4)].astype(F32)
            field = along_rows(along_lanes(field.reshape(256, 128)))
            work[pl.ds(x, 4)] = field.reshape(4, NG, 128)

    @pl.loop(0, NG // 8)
    def _(i):
        at = pl.ds(pl.multiple_of(i * 8, 8), 8)
        planes = jnp.swapaxes(work[:, at, :], 0, 1)
        done = []
        for part in range(2):
            field = planes[part * 4:part * 4 + 4].reshape(256, 128)
            field = along_rows(field) * table[pl.ds(i * 8 + part * 4, 4)].reshape(256, 128)
            done.append(along_rows(field).reshape(4, NG, 128))
        work[:, at, :] = jnp.swapaxes(jnp.concatenate(done, axis=0), 0, 1)

    for slab in range(slabs):
        @pl.loop(0, rows // 4, unroll=2)
        def _(i):
            x = slab * rows + i * 4
            field = along_lanes(along_rows(work[pl.ds(x, 4)].reshape(256, 128)))
            field = field.reshape(4, NG, 128) * partner[pl.ds(x, 4)].astype(F32)
            out[slab, 0, pl.ds(i * 4, 4)] = (-field).astype(BF)


def solve(pairs, partner):
    slabs, count, rows = pairs.shape[:3]
    matrix = cas_matrix(NG)
    left = matrix_halves(jnp.kron(jnp.eye(4, dtype=F32), matrix))
    right = matrix_halves(jnp.kron(jnp.eye(2, dtype=F32), matrix))
    right_hi = jnp.concatenate([right[0], right[0]], axis=0)
    block = pl.BlockSpec((slabs, 1, rows, NG, 128), lambda i: (0, i, 0, 0, 0))
    whole = lambda array: pl.BlockSpec(array.shape, lambda i: (0,) * array.ndim)
    fixed = (partner, kernel_table(), left[0], left[1], right_hi, right[1])
    return pl.pallas_call(
        lambda *refs: solve_body(slabs, rows, *refs),
        grid=(count,),
        in_specs=[block] + [whole(a) for a in fixed],
        out_specs=block,
        out_shape=jax.ShapeDtypeStruct(pairs.shape, BF),
        scratch_shapes=[pltpu.VMEM((NG, NG, 128), F32)],
        compiler_params=pltpu.CompilerParams(vmem_limit_bytes=48 * 1024 * 1024),
        cost_estimate=pl.CostEstimate(
            flops=count * 60 * NG * NG * 128 * 256, bytes_accessed=4 * pairs.size, transcendentals=0
        ),
    )(pairs, *fixed)


def gram_body(left, right, out):
    @pl.when(pl.program_id(0) == 0)
    def _():
        out[...] = jnp.zeros_like(out)

    size = out.shape[0]
    a = left[:, 0].reshape(size, left.shape[3])
    b = right[:, 0].reshape(size, right.shape[3])
    out[...] += lax.dot_general(a, b, (((1,), (1,)), ((), ())), preferred_element_type=F32)


def gram_product(left, right):
    shares, planes, bands, points = left.shape
    size = shares * bands
    if bands % 16 or points % 128:
        return jnp.einsum("gxbk,hxck->gbhc", left, right, preferred_element_type=F32).reshape(size, size)
    block = pl.BlockSpec((shares, 1, bands, points), lambda i: (0, i, 0, 0))
    return pl.pallas_call(
        gram_body,
        grid=(planes,),
        in_specs=[block, block],
        out_specs=pl.BlockSpec((size, size), lambda i: (0, 0)),
        out_shape=jax.ShapeDtypeStruct((size, size), F32),
        compiler_params=pltpu.CompilerParams(vmem_limit_bytes=32 * 1024 * 1024),
        cost_estimate=pl.CostEstimate(
            flops=2 * size * size * planes * points, bytes_accessed=4 * left.size, transcendentals=0
        ),
    )(left, right)


def to_shares(array):
    shares = lax.axis_size("band")
    bands, planes, square = array.shape
    cut = array.reshape(bands, planes, shares, square // shares).transpose(2, 1, 0, 3)
    return lax.all_to_all(cut, "band", split_axis=0, concat_axis=0)


def per_device(orbitals, picks):
    bands, planes, square = orbitals.shape
    groups = lax.axis_size("grid")
    pairs = bands // groups // 2
    target = picks[0]
    mine = lax.dynamic_index_in_dim(orbitals, target % bands, 0, keepdims=False)
    slab = spread(mine, "band", target // bands).reshape(planes, NG, NG)
    partner = lax.all_gather(jnp.concatenate([slab, slab], axis=2), "grid", axis=0, tiled=True)

    paired = orbitals.reshape(groups, pairs, 2, planes, NG, NG).transpose(0, 1, 3, 4, 2, 5)
    paired = paired.reshape(groups, pairs, planes, NG, 128)
    cubes = lax.all_to_all(paired, "grid", split_axis=0, concat_axis=0)
    spread_orbitals = to_shares(orbitals)
    solved = solve(cubes, partner)
    solved, spread_orbitals = lax.optimization_barrier((solved, spread_orbitals))
    back = lax.all_to_all(solved, "grid", split_axis=0, concat_axis=0)
    vectors = back.reshape(groups, pairs, planes, NG, 2, NG).transpose(0, 1, 4, 2, 3, 5)
    vectors = vectors.reshape(bands, planes, square)
    spread_vectors = to_shares(vectors)
    product = gram_product(spread_orbitals, spread_vectors)
    partial_rows = lax.psum_scatter(product * (1.0 / NPTS), "band", scatter_dimension=0, tiled=True)
    gram = lax.psum(partial_rows, "grid")
    return (vectors, gram)


def solution(mesh):
    return jax.shard_map(
        per_device,
        mesh=mesh,
        in_specs=(P("band", "grid", None), P()),
        out_specs=(P("band", "grid", None), P("band", None)),
        check_vma=False,
    )
```
